256 devices in a mesh: segment: 8 (over y, core), neuron: 32 (over z, x).
Axes of the slice: x: 4, y: 4, z: 8, core: 2. Of those that a mesh axis runs over, the one named last changes fastest.
Arguments:
- samples: bfloat16 [384, 65536], P(None, 'neuron'), may hold values from -6 to 6
- batch_of: int32 [384], replicated, may hold values from 0 to 2, as said below
- weights: bfloat16 [16, 512, 5, 128, 128], P('segment', 'neuron'), may hold values from -0.375 to 0.375
- block_offset: int32 [16, 512, 5], P('segment', 'neuron'), may hold values from -4 to 4, as said below
- block_count: int32 [16, 512], P('segment', 'neuron'), may hold values from 3 to 5
- bias: float32 [16, 65536], P('segment', 'neuron'), may hold values from -0.4 to 0.2
Outputs:
- section_out: bfloat16 [8, 3, 128, 65536], P('segment', None, None, 'neuron')
The draws below stay inside these ranges and needn't reach their ends.
Inputs may be any that keep to these rules, and one draw needn't show every extreme that they name: `block_offset`: the 5 offsets of one block row are distinct. `batch_of`: each of the 3 micro-batches holds exactly 128 samples.
All inputs are finite; a program needn't handle non-finite values.
Results may differ from the reference program's by a relative error of at most 0.029.
Values may be sent and summed in bfloat16 or wider, within the bound.
A program may use at most 64 MiB of HBM per device.

```python
import jax
import jax.numpy as jnp

N = 65536
BLOCK = 128
KMAX = 5
REACH = 4
LPS = 2
S = 128
NMB = 3
NBR = 512
LAYERS = 16
SAMPLES = 384


def draw_batch_of(key, part):
    key = jax.random.fold_in(key, 11)
    return (jax.random.permutation(key, SAMPLES) // S).astype(jnp.int32)


def draw_block_offset(key, part):
    key = jax.random.fold_in(key, 23)
    choices_total = 2 * REACH + 1
    scores = jax.random.randint(key, (LAYERS, NBR, choices_total), 0, 1 << 20) * choices_total
    scores = scores + jnp.arange(choices_total, dtype=jnp.int32)
    ranked = jnp.argsort(scores, axis=-1)[..., :KMAX]
    return (ranked - REACH).astype(jnp.int32)


def place_ends(drawn, rng, smallest, high):
    dims = drawn.shape
    place = [jax.random.randint(jax.random.fold_in(rng, axis), (), 0, dims[axis]) for axis in range(len(dims))]
    drawn = drawn.at[tuple(place)].set(smallest)
    longest = dims.index(max(dims))
    place[longest] = (place[longest] + 1) % dims[longest]
    return drawn.at[tuple(place)].set(high)


def level_of(rng, shape, split, low, high):
    gain = 1.0
    for position, blocks in split:
        heights = jax.random.uniform(jax.random.fold_in(jax.random.fold_in(rng, 6), position), (blocks,), jnp.float32, low / len(split), high / len(split))
        gain = gain * jnp.repeat(jnp.exp(heights), shape[position] // blocks).reshape((-1,) + (1,) * (len(shape) - 1 - position))
    return gain


def bell_draw(key, dims, width, bound, pieces=(), kind=jnp.bfloat16):
    level = level_of(key, dims, pieces, -0.22, 0.18) if pieces else 1.0
    values = jax.random.normal(key, dims, jnp.float32) * width * level
    return jnp.minimum(jnp.maximum(values, -bound), bound).astype(kind)


def setup_inputs(seed: int = 0) -> dict:
    arg_keys = jax.random.split(jax.random.key(seed), 7)
    samples = bell_draw(arg_keys[0], (SAMPLES, N), 1.0, 6.0, ((1, 32),))
    batch_of = draw_batch_of(jax.random.fold_in(arg_keys[6], 71), 0)
    weights = bell_draw(arg_keys[2], (LAYERS, NBR, KMAX, BLOCK, BLOCK), (48 * KMAX) ** -0.5, 0.375, ((0, 8), (1, 32)))
    block_offset = draw_block_offset(jax.random.fold_in(arg_keys[6], 71), 0)
    block_count = place_ends(jax.random.randint(arg_keys[4], (LAYERS, NBR), 3, 6), jax.random.fold_in(arg_keys[4], 1), 3, 5).astype(jnp.int32)
    bias = jnp.clip(-0.4 + 0.6 * jax.random.uniform(arg_keys[5], (LAYERS, N), jnp.float32) ** level_of(arg_keys[5], (LAYERS, N), ((0, 8), (1, 32)), -0.2, 0.2), -0.4, 0.2)
    return dict(samples=samples, batch_of=batch_of, weights=weights, block_offset=block_offset, block_count=block_count, bias=bias)


def apply_layer(current, weight, offset, count, bias_row):
    row_count = current.shape[0]
    block_total = weight.shape[0]
    padded = jnp.pad(current, ((0, 0), (REACH * BLOCK, REACH * BLOCK)))
    blocks = padded.reshape(row_count, block_total + 2 * REACH, BLOCK)
    slot_index = (jnp.arange(block_total, dtype=jnp.int32)[:, None] + REACH + offset).astype(jnp.int32)
    picked = jnp.take(blocks, slot_index.reshape(-1), axis=1).reshape(row_count, block_total, KMAX, BLOCK)
    live_slots = jnp.arange(KMAX, dtype=jnp.int32)[None, :] < count[:, None]
    picked = jnp.where(live_slots[None, :, :, None], picked, jnp.zeros((), picked.dtype))
    summed = jnp.einsum("rjkc,jkcd->rjd", picked.astype(jnp.float32), weight.astype(jnp.float32))
    summed = summed.reshape(row_count, block_total * BLOCK)
    return jnp.maximum(summed + bias_row[None, :], 0.0).astype(jnp.bfloat16)


def reference(samples, batch_of, weights, block_offset, block_count, bias):
    order = jnp.argsort(batch_of, stable=True).astype(jnp.int32).reshape(NMB, S)
    results = []
    for batch_no in range(NMB):
        current = jnp.take(samples, order[batch_no], axis=0)
        sections = []
        for layer_no in range(LAYERS):
            current = apply_layer(current, weights[layer_no], block_offset[layer_no], block_count[layer_no], bias[layer_no])
            if (layer_no + 1) % LPS == 0:
                sections.append(current)
        results.append(jnp.stack(sections))
    return jnp.stack(results, axis=1)
```

```python
import functools

import jax
import jax.numpy as jnp
from jax import lax
from jax.experimental import pallas as pl
from jax.experimental.pallas import tpu as pltpu
from jax.sharding import PartitionSpec as P

MESH = pl.DeviceIdType.MESH
BLOCK = 128
KMAX = 5
REACH = 4
S = 128
NMB = 3
ROWS = 16
WIDE = 2 * REACH
EDGE = ROWS + 2 * REACH
XZERO = ROWS + 2 * WIDE
HZERO = EDGE
HSTEP = EDGE + 1
HALF = ROWS // 2
SAMPLES = S * NMB


def kernel(
    segments, neurons, piece,
    samples, batch, weights, bias_any, offset_any, count_any, bias, offset, count,
    out,
    wa, wb, raw, main, halo, mid, mid_out, result, x, h, bias_l, bias_r,
    off_l, off_r, cnt_l, cnt_r, ia, ib, pos,
    load_sem, info_send, info_recv, w_send, w_recv,
    main_send, main_recv, halo_send, halo_recv, fwd_send, mid_send, mid_recv, out_sem,
):
    pieces = SAMPLES // piece
    s = lax.axis_index("segment")
    n = lax.axis_index("neuron")
    left = lax.rem(n + neurons - 1, neurons)
    right = lax.rem(n + 1, neurons)
    odd = lax.rem(s, 2)
    first = s == 0
    even = odd == 0
    last = s == segments - 1
    pair = s + 1 - 2 * odd
    crossing = jnp.logical_not(first) & jnp.logical_not(last)
    other = jnp.clip(s - 1 + 2 * odd, 0, segments - 1)

    def remote(src, dst, send, recv, device):
        return pltpu.make_async_remote_copy(
            src_ref=src, dst_ref=dst, send_sem=send, recv_sem=recv,
            device_id=device, device_id_type=MESH,
        )

    load_a = pltpu.make_async_copy(weights.at[0], wa.at[pl.ds(REACH, ROWS)], load_sem.at[0])
    load_b = pltpu.make_async_copy(weights.at[1], wb, load_sem.at[1])
    load_s = pltpu.make_async_copy(samples, raw, load_sem.at[2])
    pl.when(first)(load_s.start)
    load_a.start()
    load_b.start()

    barrier = pltpu.get_barrier_semaphore()

    def greet(device):
        pl.semaphore_signal(barrier, inc=1, device_id=device, device_id_type=MESH)

    greet((s, left))
    greet((s, right))
    greet((pair, n))
    greet((pair, left))
    greet((pair, right))
    pl.when(crossing)(lambda: greet((other, n)))

    x[XZERO] = jnp.zeros((piece, BLOCK), jnp.bfloat16)
    for slot in range(2):
        h[slot * HSTEP + HZERO] = jnp.zeros((piece, BLOCK), jnp.bfloat16)

    @pl.when(first)
    def _():
        lanes = lax.broadcasted_iota(jnp.int32, (8, SAMPLES), 0)
        hot = jnp.where(jnp.broadcast_to(batch[...], (8, SAMPLES)) == lanes, 1.0, 0.0)
        before = jnp.where(
            lax.broadcasted_iota(jnp.int32, (SAMPLES, SAMPLES), 0)
            < lax.broadcasted_iota(jnp.int32, (SAMPLES, SAMPLES), 1),
            1.0, 0.0,
        ).astype(jnp.bfloat16)
        rank = jnp.dot(hot.astype(jnp.bfloat16), before, preferred_element_type=jnp.float32)
        place = hot * (rank + lanes.astype(jnp.float32) * float(S))
        pos[...] = jnp.broadcast_to(jnp.sum(place, axis=0, keepdims=True), (8, SAMPLES))

    pl.semaphore_wait(barrier, jnp.where(crossing, 6, 5))

    info = [
        remote(offset_any, off_r, info_send.at[0], info_recv.at[0], (s, left)),
        remote(offset_any, off_l, info_send.at[1], info_recv.at[1], (s, right)),
        remote(count_any, cnt_r, info_send.at[2], info_recv.at[2], (s, left)),
        remote(count_any, cnt_l, info_send.at[3], info_recv.at[3], (s, right)),
        remote(bias_any, bias_r, info_send.at[4], info_recv.at[4], (s, left)),
        remote(bias_any, bias_l, info_send.at[5], info_recv.at[5], (s, right)),
    ]
    rows_of_neighbours = [
        remote(
            weights.at[0, pl.ds(0, REACH)], wa.at[pl.ds(REACH + ROWS, REACH)],
            w_send.at[0], w_recv.at[0], (s, left),
        ),
        remote(
            weights.at[0, pl.ds(ROWS - REACH, REACH)], wa.at[pl.ds(0, REACH)],
            w_send.at[1], w_recv.at[1], (s, right),
        ),
    ]

    @pl.when(jnp.logical_not(first))
    def _():
        for copy in info:
            copy.start()
        for copy in rows_of_neighbours:
            copy.start()

    def main_copy(p, half, device):
        cols = pl.ds(half * HALF * BLOCK, HALF * BLOCK)
        return remote(
            result.at[p, :, cols], main.at[p, :, cols],
            main_send.at[p, half], main_recv.at[p, half], device,
        )

    def halo_copy(p, half, device):
        cols = pl.ds(half * HALF * BLOCK, HALF * BLOCK)
        return remote(
            result.at[p, :, cols], halo.at[p, 1 - half],
            halo_send.at[p, half], halo_recv.at[p, 1 - half], device,
        )

    def fwd_copy(p, half, device):
        cols = pl.ds(half * HALF * BLOCK, HALF * BLOCK)
        return remote(
            main.at[p, :, cols], halo.at[p, 1 - half],
            fwd_send.at[p, half], halo_recv.at[p, 1 - half], device,
        )

    def narrow_copy(p, half, device):
        width = REACH * BLOCK
        src = pl.ds(half * (ROWS - REACH) * BLOCK, width)
        dst = pl.ds((1 - half) * 0 + half * REACH * BLOCK, width)
        return remote(
            main.at[p, :, src], halo.at[p, 1 - half, :, dst],
            fwd_send.at[p, half], halo_recv.at[p, 1 - half], device,
        )

    def mid_copy(p, half, device):
        return remote(
            mid_out.at[p, half], mid.at[p, 1 - half],
            mid_send.at[p, half], mid_recv.at[p, 1 - half], device,
        )

    sides = ((0, (s, left)), (1, (s, right)))
    pair_sides = ((0, (pair, left)), (1, (pair, right)))

    def prepare(p):
        @pl.when(first)
        def _():
            want = lax.broadcasted_iota(jnp.int32, (piece, SAMPLES), 0) + p * piece
            pick = jnp.where(
                jnp.broadcast_to(pos[0:1, :], (piece, SAMPLES)) == want.astype(jnp.float32),
                1.0, 0.0,
            ).astype(jnp.bfloat16)
            for c in range(0, ROWS * BLOCK, 2 * BLOCK):
                main[p, :, c : c + 2 * BLOCK] = jnp.dot(
                    pick, raw[:, c : c + 2 * BLOCK], preferred_element_type=jnp.float32
                ).astype(jnp.bfloat16)
            for half, device in sides:
                narrow_copy(p, half, device).start()

        @pl.when(jnp.logical_not(first))
        def _():
            for half, device in sides:
                main_copy(p, half, (s, n)).wait_recv()
                fwd_copy(p, half, device).start()

    def first_rows(rows, slot, keep):
        for a in rows:
            taken = jnp.concatenate([x[ia[a * KMAX + k]] for k in range(KMAX)], axis=1)
            y = jnp.dot(
                taken, wa[a].reshape(KMAX * BLOCK, BLOCK), preferred_element_type=jnp.float32
            )
            j = a - REACH
            if j < 0:
                b = bias_l[0:1, (j + ROWS) * BLOCK : (j + ROWS + 1) * BLOCK]
            elif j < ROWS:
                b = bias[0:1, j * BLOCK : (j + 1) * BLOCK]
            else:
                b = bias_r[0:1, (j - ROWS) * BLOCK : (j - ROWS + 1) * BLOCK]
            y = jnp.maximum(y + b, 0.0).astype(jnp.bfloat16)
            h[slot * HSTEP + a] = y
            if keep is not None:
                keep(j, y)

    def second_rows(rows, slot, p):
        for j in rows:
            taken = jnp.concatenate(
                [h[slot * HSTEP + ib[j * KMAX + k]] for k in range(KMAX)], axis=1
            )
            y = jnp.dot(
                taken, wb[j].reshape(KMAX * BLOCK, BLOCK), preferred_element_type=jnp.float32
            )
            b = bias[1:2, j * BLOCK : (j + 1) * BLOCK]
            result[p, :, j * BLOCK : (j + 1) * BLOCK] = jnp.maximum(y + b, 0.0).astype(jnp.bfloat16)

    def stage_a(p):
        slot = lax.rem(p, 2)

        @pl.when(jnp.logical_not(even))
        def _():
            for half, _ in sides:
                main_copy(p, half, (pair, n)).wait_recv()

        for j in range(ROWS):
            x[WIDE + j] = main[p, :, j * BLOCK : (j + 1) * BLOCK]
        first_rows(range(2 * REACH, EDGE - 2 * REACH), slot, None)

        @pl.when(first)
        def _():
            for half, device in sides:
                narrow_copy(p, half, device).wait_recv()
            for j in range(REACH):
                c = (REACH + j) * BLOCK
                x[REACH + j] = halo[p, 0, :, c : c + BLOCK]
                x[WIDE + ROWS + j] = halo[p, 1, :, j * BLOCK : (j + 1) * BLOCK]

            def keep(j, y):
                half = 0 if j < REACH else 1
                c = (j - half * (ROWS - REACH)) * BLOCK
                mid_out[p, half, :, c : c + BLOCK] = y

            first_rows(range(REACH, 2 * REACH), slot, keep)
            first_rows(range(EDGE - 2 * REACH, EDGE - REACH), slot, keep)
            for half, device in sides:
                mid_copy(p, half, device).start()

        @pl.when(jnp.logical_not(first))
        def _():
            for half, device in sides:
                fwd_copy(p, half, device).wait_recv()
            for j in range(WIDE):
                x[j] = halo[p, 0, :, j * BLOCK : (j + 1) * BLOCK]
                x[WIDE + ROWS + j] = halo[p, 1, :, j * BLOCK : (j + 1) * BLOCK]
            first_rows(range(2 * REACH), slot, None)
            first_rows(range(EDGE - 2 * REACH, EDGE), slot, None)

    def stage_b(p):
        slot = lax.rem(p, 2)

        @pl.when(first)
        def _():
            for half, device in sides:
                mid_copy(p, half, device).wait_recv()
            for j in range(REACH):
                h[slot * HSTEP + j] = mid[p, 0, :, j * BLOCK : (j + 1) * BLOCK]
                h[slot * HSTEP + REACH + ROWS + j] = mid[p, 1, :, j * BLOCK : (j + 1) * BLOCK]

        for half in range(2):
            second_rows(range(half * HALF, (half + 1) * HALF), slot, p)

            @pl.when(even)
            def _():
                halo_copy(p, half, pair_sides[half][1]).start()
                main_copy(p, half, (pair, n)).start()

            @pl.when(jnp.logical_not(even) & jnp.logical_not(last))
            def _():
                main_copy(p, half, (other, n)).start()

        out_copy(p).start()

    def out_copy(p):
        return pltpu.make_async_copy(
            result.at[p], out.at[pl.ds(p * piece, piece), :], out_sem.at[p]
        )

    def fill(table, entry, off_ref, cnt_ref, layer, row, j, base, zero):
        used = cnt_ref[layer, row]
        for k in range(KMAX):
            off = off_ref[layer, row, k]
            place = n * ROWS + j + off
            live = (k < used) & (place >= 0) & (place < neurons * ROWS)
            table[entry * KMAX + k] = jnp.where(live, base + j + off, zero)

    def own(r, carry):
        fill(ia, r + REACH, offset, count, 0, r, r, WIDE, XZERO)
        fill(ib, r, offset, count, 1, r, r, REACH, HZERO)
        return carry

    lax.fori_loop(0, ROWS, own, 0)
    pl.when(first)(load_s.wait)
    pl.when(even)(lambda: prepare(0))

    @pl.when(jnp.logical_not(first))
    def _():
        for copy in info:
            copy.wait_recv()

        def sides_rows(r, carry):
            fill(ia, r, off_l, cnt_l, 0, ROWS - REACH + r, r - REACH, WIDE, XZERO)
            fill(ia, r + REACH + ROWS, off_r, cnt_r, 0, r, r + ROWS, WIDE, XZERO)
            return carry

        lax.fori_loop(0, REACH, sides_rows, 0)
        for copy in rows_of_neighbours:
            copy.wait_recv()

    load_a.wait()
    load_b.wait()

    def step(q, carry):
        @pl.when(q < pieces)
        def _():
            pl.when(even & (q + 1 < pieces))(lambda: prepare(q + 1))
            stage_a(q)

        p = q - jnp.where(first, 1, 0)
        pl.when((p >= 0) & (p < pieces))(lambda: stage_b(p))
        return carry

    lax.fori_loop(0, pieces + 1, step, 0)

    @pl.when(jnp.logical_not(first))
    def _():
        for copy in info:
            copy.wait_send()
        for copy in rows_of_neighbours:
            copy.wait_send()

    def drain(p, carry):
        out_copy(p).wait()
        for half in range(2):
            pl.when(jnp.logical_not(last))(lambda: main_copy(p, half, (pair, n)).wait_send())
            pl.when(even)(lambda: halo_copy(p, half, pair_sides[half][1]).wait_send())
            pl.when(first)(lambda: narrow_copy(p, half, sides[half][1]).wait_send())
            pl.when(first)(lambda: mid_copy(p, half, sides[half][1]).wait_send())
            pl.when(even & jnp.logical_not(first))(
                lambda: fwd_copy(p, half, sides[half][1]).wait_send()
            )
        return carry

    lax.fori_loop(0, pieces, drain, 0)


def solution(mesh):
    segments, neurons = mesh.shape["segment"], mesh.shape["neuron"]
    piece = 48
    pieces = SAMPLES // piece
    width = ROWS * BLOCK
    bf16, f32, i32 = jnp.bfloat16, jnp.float32, jnp.int32

    def on_device(samples, batch_of, weights, block_offset, block_count, bias):
        dma = pltpu.SemaphoreType.DMA
        vmem = pl.BlockSpec(memory_space=pltpu.VMEM)
        smem = pl.BlockSpec(memory_space=pltpu.SMEM)
        hbm = pl.BlockSpec(memory_space=pl.ANY)
        result = pl.pallas_call(
            functools.partial(kernel, segments, neurons, piece),
            out_shape=jax.ShapeDtypeStruct((SAMPLES, width), bf16),
            in_specs=[hbm, vmem, hbm, hbm, hbm, hbm, vmem, smem, smem],
            out_specs=hbm,
            scratch_shapes=[
                pltpu.VMEM((EDGE, KMAX, BLOCK, BLOCK), bf16),
                pltpu.VMEM((ROWS, KMAX, BLOCK, BLOCK), bf16),
                pltpu.VMEM((SAMPLES, width), bf16),
                pltpu.VMEM((pieces, piece, width), bf16),
                pltpu.VMEM((pieces, 2, piece, WIDE * BLOCK), bf16),
                pltpu.VMEM((pieces, 2, piece, REACH * BLOCK), bf16),
                pltpu.VMEM((pieces, 2, piece, REACH * BLOCK), bf16),
                pltpu.VMEM((pieces, piece, width), bf16),
                pltpu.VMEM((XZERO + 1, piece, BLOCK), bf16),
                pltpu.VMEM((2 * HSTEP, piece, BLOCK), bf16),
                pltpu.VMEM(bias.shape, f32),
                pltpu.VMEM(bias.shape, f32),
                pltpu.SMEM(block_offset.shape, i32),
                pltpu.SMEM(block_offset.shape, i32),
                pltpu.SMEM(block_count.shape, i32),
                pltpu.SMEM(block_count.shape, i32),
                pltpu.SMEM((EDGE * KMAX,), i32),
                pltpu.SMEM((ROWS * KMAX,), i32),
                pltpu.VMEM((8, SAMPLES), f32),
                dma((3,)), dma((6,)), dma((6,)), dma((2,)), dma((2,)),
                dma((pieces, 2)), dma((pieces, 2)), dma((pieces, 2)), dma((pieces, 2)),
                dma((pieces, 2)), dma((pieces, 2)), dma((pieces, 2)), dma((pieces,)),
            ],
            compiler_params=pltpu.CompilerParams(
                collective_id=0, has_side_effects=True, vmem_limit_bytes=56 << 20
            ),
        )(
            samples, batch_of.reshape(1, SAMPLES), weights, bias, block_offset, block_count,
            bias, block_offset, block_count,
        )
        return result.reshape(1, NMB, S, width)

    return jax.shard_map(
        on_device,
        mesh=mesh,
        in_specs=(
            P(None, "neuron"),
            P(),
            P("segment", "neuron", None, None, None),
            P("segment", "neuron", None),
            P("segment", "neuron"),
            P("segment", "neuron"),
        ),
        out_specs=P("segment", None, None, "neuron"),
        check_vma=False,
    )
```

```python
import functools

import jax
import jax.numpy as jnp
from jax import lax
from jax.experimental import pallas as pl
from jax.experimental.pallas import tpu as pltpu
from jax.sharding import PartitionSpec as P

MESH = pl.DeviceIdType.MESH
BLOCK = 128
KMAX = 5
REACH = 4
S = 128
NMB = 3
ROWS = 16
WIDE = 2 * REACH
EDGE = ROWS + 2 * REACH
XZERO = ROWS + 2 * WIDE
HZERO = EDGE
HSTEP = EDGE + 1
HALF = ROWS // 2
SAMPLES = S * NMB
AHEAD = 2
LAG = 2
SLOTS = LAG + 1


def kernel(
    segments, neurons, piece,
    samples, batch, weights, bias_any, offset_any, count_any, bias, offset, count,
    out,
    wa, wb, raw, main, halo, mid, mid_out, result, x, h, bias_l, bias_r,
    off_l, off_r, cnt_l, cnt_r, ia, ib, pos,
    load_sem, info_send, info_recv, w_send, w_recv,
    main_send, main_recv, halo_send, halo_recv, fwd_send, mid_send, mid_recv, out_sem,
):
    pieces = SAMPLES // piece
    s = lax.axis_index("segment")
    n = lax.axis_index("neuron")
    left = lax.rem(n + neurons - 1, neurons)
    right = lax.rem(n + 1, neurons)
    odd = lax.rem(s, 2)
    first = s == 0
    even = odd == 0
    last = s == segments - 1
    pair = s + 1 - 2 * odd
    crossing = jnp.logical_not(first) & jnp.logical_not(last)
    other = jnp.clip(s - 1 + 2 * odd, 0, segments - 1)

    def remote(src, dst, send, recv, device):
        return pltpu.make_async_remote_copy(
            src_ref=src, dst_ref=dst, send_sem=send, recv_sem=recv,
            device_id=device, device_id_type=MESH,
        )

    load_a = pltpu.make_async_copy(weights.at[0], wa.at[pl.ds(REACH, ROWS)], load_sem.at[0])
    load_b = pltpu.make_async_copy(weights.at[1], wb, load_sem.at[1])
    load_s = pltpu.make_async_copy(samples, raw, load_sem.at[2])
    pl.when(first)(load_s.start)
    load_a.start()
    load_b.start()

    barrier = pltpu.get_barrier_semaphore()

    def greet(device):
        pl.semaphore_signal(barrier, inc=1, device_id=device, device_id_type=MESH)

    greet((s, left))
    greet((s, right))
    greet((pair, n))
    greet((pair, left))
    greet((pair, right))
    pl.when(crossing)(lambda: greet((other, n)))

    x[XZERO] = jnp.zeros((piece, BLOCK), jnp.bfloat16)
    for slot in range(SLOTS):
        h[slot * HSTEP + HZERO] = jnp.zeros((piece, BLOCK), jnp.bfloat16)

    @pl.when(first)
    def _():
        lanes = lax.broadcasted_iota(jnp.int32, (8, SAMPLES), 0)
        hot = jnp.where(jnp.broadcast_to(batch[...].reshape(1, SAMPLES), (8, SAMPLES)) == lanes, 1.0, 0.0)
        before = jnp.where(
            lax.broadcasted_iota(jnp.int32, (SAMPLES, SAMPLES), 0)
            < lax.broadcasted_iota(jnp.int32, (SAMPLES, SAMPLES), 1),
            1.0, 0.0,
        ).astype(jnp.bfloat16)
        rank = jnp.dot(hot.astype(jnp.bfloat16), before, preferred_element_type=jnp.float32)
        place = hot * (rank + lanes.astype(jnp.float32) * float(S))
        pos[...] = jnp.broadcast_to(jnp.sum(place, axis=0, keepdims=True), (8, SAMPLES))

    pl.semaphore_wait(barrier, jnp.where(crossing, 6, 5))

    info = [
        remote(offset_any, off_r, info_send.at[0], info_recv.at[0], (s, left)),
        remote(offset_any, off_l, info_send.at[1], info_recv.at[1], (s, right)),
        remote(count_any, cnt_r, info_send.at[2], info_recv.at[2], (s, left)),
        remote(count_any, cnt_l, info_send.at[3], info_recv.at[3], (s, right)),
        remote(bias_any, bias_r, info_send.at[4], info_recv.at[4], (s, left)),
        remote(bias_any, bias_l, info_send.at[5], info_recv.at[5], (s, right)),
    ]
    rows_of_neighbours = [
        remote(
            weights.at[0, pl.ds(0, REACH)], wa.at[pl.ds(REACH + ROWS, REACH)],
            w_send.at[0], w_recv.at[0], (s, left),
        ),
        remote(
            weights.at[0, pl.ds(ROWS - REACH, REACH)], wa.at[pl.ds(0, REACH)],
            w_send.at[1], w_recv.at[1], (s, right),
        ),
    ]

    @pl.when(jnp.logical_not(first))
    def _():
        for copy in info:
            copy.start()
        for copy in rows_of_neighbours:
            copy.start()

    def main_copy(p, half, device):
        cols = pl.ds(half * HALF * BLOCK, HALF * BLOCK)
        return remote(
            result.at[p, :, cols], main.at[p, :, cols],
            main_send.at[p, half], main_recv.at[p, half], device,
        )

    def halo_copy(p, half, device):
        cols = pl.ds(half * HALF * BLOCK, HALF * BLOCK)
        return remote(
            result.at[p, :, cols], halo.at[p, 1 - half],
            halo_send.at[p, half], halo_recv.at[p, 1 - half], device,
        )

    def fwd_copy(p, half, device):
        cols = pl.ds(half * HALF * BLOCK, HALF * BLOCK)
        return remote(
            main.at[p, :, cols], halo.at[p, 1 - half],
            fwd_send.at[p, half], halo_recv.at[p, 1 - half], device,
        )

    def narrow_copy(p, half, device):
        width = REACH * BLOCK
        src = pl.ds(half * (ROWS - REACH) * BLOCK, width)
        dst = pl.ds((1 - half) * 0 + half * REACH * BLOCK, width)
        return remote(
            main.at[p, :, src], halo.at[p, 1 - half, :, dst],
            fwd_send.at[p, half], halo_recv.at[p, 1 - half], device,
        )

    def mid_copy(p, half, device):
        return remote(
            mid_out.at[p, half], mid.at[p, 1 - half],
            mid_send.at[p, half], mid_recv.at[p, 1 - half], device,
        )

    sides = ((0, (s, left)), (1, (s, right)))
    pair_sides = ((0, (pair, left)), (1, (pair, right)))

    def prepare(p):
        @pl.when(first)
        def _():
            want = lax.broadcasted_iota(jnp.int32, (piece, SAMPLES), 0) + p * piece
            pick = jnp.where(
                jnp.broadcast_to(pos[0:1, :], (piece, SAMPLES)) == want.astype(jnp.float32),
                1.0, 0.0,
            ).astype(jnp.bfloat16)
            for c in range(0, ROWS * BLOCK, 2 * BLOCK):
                main[p, :, c : c + 2 * BLOCK] = jnp.dot(
                    pick, raw[:, c : c + 2 * BLOCK], preferred_element_type=jnp.float32
                ).astype(jnp.bfloat16)
            for half, device in sides:
                narrow_copy(p, half, device).start()

        @pl.when(jnp.logical_not(first))
        def _():
            for half, device in sides:
                main_copy(p, half, (s, n)).wait_recv()
                fwd_copy(p, half, device).start()

    def first_rows(rows, slot, keep):
        for a in rows:
            taken = jnp.concatenate([x[ia[a * KMAX + k]] for k in range(KMAX)], axis=1)
            y = jnp.dot(
                taken, wa[a].reshape(KMAX * BLOCK, BLOCK), preferred_element_type=jnp.float32
            )
            j = a - REACH
            if j < 0:
                b = bias_l[0:1, (j + ROWS) * BLOCK : (j + ROWS + 1) * BLOCK]
            elif j < ROWS:
                b = bias[0:1, j * BLOCK : (j + 1) * BLOCK]
            else:
                b = bias_r[0:1, (j - ROWS) * BLOCK : (j - ROWS + 1) * BLOCK]
            y = jnp.maximum(y + b, 0.0).astype(jnp.bfloat16)
            h[slot * HSTEP + a] = y
            if keep is not None:
                keep(j, y)

    def second_rows(rows, slot, p):
        for j in rows:
            taken = jnp.concatenate(
                [h[slot * HSTEP + ib[j * KMAX + k]] for k in range(KMAX)], axis=1
            )
            y = jnp.dot(
                taken, wb[j].reshape(KMAX * BLOCK, BLOCK), preferred_element_type=jnp.float32
            )
            b = bias[1:2, j * BLOCK : (j + 1) * BLOCK]
            result[p, :, j * BLOCK : (j + 1) * BLOCK] = jnp.maximum(y + b, 0.0).astype(jnp.bfloat16)

    def stage_a(p):
        slot = lax.rem(p, SLOTS)

        @pl.when(jnp.logical_not(even))
        def _():
            for half, _ in sides:
                main_copy(p, half, (pair, n)).wait_recv()

        for j in range(ROWS):
            x[WIDE + j] = main[p, :, j * BLOCK : (j + 1) * BLOCK]
        first_rows(range(2 * REACH, EDGE - 2 * REACH), slot, None)

        @pl.when(first)
        def _():
            for half, device in sides:
                narrow_copy(p, half, device).wait_recv()
            for j in range(REACH):
                c = (REACH + j) * BLOCK
                x[REACH + j] = halo[p, 0, :, c : c + BLOCK]
                x[WIDE + ROWS + j] = halo[p, 1, :, j * BLOCK : (j + 1) * BLOCK]

            def keep(j, y):
                half = 0 if j < REACH else 1
                c = (j - half * (ROWS - REACH)) * BLOCK
                mid_out[p, half, :, c : c + BLOCK] = y

            first_rows(range(REACH, 2 * REACH), slot, keep)
            first_rows(range(EDGE - 2 * REACH, EDGE - REACH), slot, keep)
            for half, device in sides:
                mid_copy(p, half, device).start()

        @pl.when(jnp.logical_not(first))
        def _():
            for half, device in sides:
                fwd_copy(p, half, device).wait_recv()
            for j in range(WIDE):
                x[j] = halo[p, 0, :, j * BLOCK : (j + 1) * BLOCK]
                x[WIDE + ROWS + j] = halo[p, 1, :, j * BLOCK : (j + 1) * BLOCK]
            first_rows(range(2 * REACH), slot, None)
            first_rows(range(EDGE - 2 * REACH, EDGE), slot, None)

    def stage_b(p):
        slot = lax.rem(p, SLOTS)

        @pl.when(first)
        def _():
            for half, device in sides:
                mid_copy(p, half, device).wait_recv()
            for j in range(REACH):
                h[slot * HSTEP + j] = mid[p, 0, :, j * BLOCK : (j + 1) * BLOCK]
                h[slot * HSTEP + REACH + ROWS + j] = mid[p, 1, :, j * BLOCK : (j + 1) * BLOCK]

        for half in range(2):
            second_rows(range(half * HALF, (half + 1) * HALF), slot, p)

            @pl.when(even)
            def _():
                halo_copy(p, half, pair_sides[half][1]).start()
                main_copy(p, half, (pair, n)).start()

            @pl.when(jnp.logical_not(even) & jnp.logical_not(last))
            def _():
                main_copy(p, half, (other, n)).start()

        out_copy(p).start()

    def out_copy(p):
        return pltpu.make_async_copy(
            result.at[p], out.at[pl.ds(p * piece, piece), :], out_sem.at[p]
        )

    def fill(table, entry, off_ref, cnt_ref, layer, row, j, base, zero):
        used = cnt_ref[layer, row]
        for k in range(KMAX):
            off = off_ref[k, layer, row]
            place = n * ROWS + j + off
            live = (k < used) & (place >= 0) & (place < neurons * ROWS)
            table[entry * KMAX + k] = jnp.where(live, base + j + off, zero)

    def own(r, carry):
        fill(ia, r + REACH, offset, count, 0, r, r, WIDE, XZERO)
        fill(ib, r, offset, count, 1, r, r, REACH, HZERO)
        return carry

    @pl.when(first)
    def _():
        load_s.wait()
        for p in range(AHEAD):
            prepare(p)

    lax.fori_loop(0, ROWS, own, 0)

    @pl.when(jnp.logical_not(first))
    def _():
        for copy in info:
            copy.wait_recv()

        def sides_rows(r, carry):
            fill(ia, r, off_l, cnt_l, 0, ROWS - REACH + r, r - REACH, WIDE, XZERO)
            fill(ia, r + REACH + ROWS, off_r, cnt_r, 0, r, r + ROWS, WIDE, XZERO)
            return carry

        lax.fori_loop(0, REACH, sides_rows, 0)
        for copy in rows_of_neighbours:
            copy.wait_recv()

    load_a.wait()
    load_b.wait()

    @pl.when(even & jnp.logical_not(first))
    def _():
        for p in range(AHEAD):
            prepare(p)

    def step(q, carry):
        @pl.when(q < pieces)
        def _():
            pl.when(even & (q + AHEAD < pieces))(lambda: prepare(q + AHEAD))
            stage_a(q)

        p = q - jnp.where(first, LAG, 0)
        pl.when((p >= 0) & (p < pieces))(lambda: stage_b(p))
        return carry

    lax.fori_loop(0, pieces + LAG, step, 0)

    @pl.when(jnp.logical_not(first))
    def _():
        for copy in info:
            copy.wait_send()
        for copy in rows_of_neighbours:
            copy.wait_send()

    def drain(p, carry):
        out_copy(p).wait()
        for half in range(2):
            pl.when(jnp.logical_not(last))(lambda: main_copy(p, half, (pair, n)).wait_send())
            pl.when(even)(lambda: halo_copy(p, half, pair_sides[half][1]).wait_send())
            pl.when(first)(lambda: narrow_copy(p, half, sides[half][1]).wait_send())
            pl.when(first)(lambda: mid_copy(p, half, sides[half][1]).wait_send())
            pl.when(even & jnp.logical_not(first))(
                lambda: fwd_copy(p, half, sides[half][1]).wait_send()
            )
        return carry

    lax.fori_loop(0, pieces, drain, 0)


def solution(mesh):
    segments, neurons = mesh.shape["segment"], mesh.shape["neuron"]
    piece = 48
    pieces = SAMPLES // piece
    width = ROWS * BLOCK
    bf16, f32, i32 = jnp.bfloat16, jnp.float32, jnp.int32

    def on_device(samples, batch_of, weights, block_offset, block_count, bias):
        dma = pltpu.SemaphoreType.DMA
        vmem = pl.BlockSpec(memory_space=pltpu.VMEM)
        smem = pl.BlockSpec(memory_space=pltpu.SMEM)
        hbm = pl.BlockSpec(memory_space=pl.ANY)
        offset = block_offset.transpose(2, 0, 1)
        result = pl.pallas_call(
            functools.partial(kernel, segments, neurons, piece),
            out_shape=jax.ShapeDtypeStruct((SAMPLES, width), bf16),
            in_specs=[hbm, vmem, hbm, hbm, hbm, hbm, vmem, smem, smem],
            out_specs=hbm,
            scratch_shapes=[
                pltpu.VMEM((EDGE, KMAX, BLOCK, BLOCK), bf16),
                pltpu.VMEM((ROWS, KMAX, BLOCK, BLOCK), bf16),
                pltpu.VMEM((SAMPLES, width), bf16),
                pltpu.VMEM((pieces, piece, width), bf16),
                pltpu.VMEM((pieces, 2, piece, WIDE * BLOCK), bf16),
                pltpu.VMEM((pieces, 2, piece, REACH * BLOCK), bf16),
                pltpu.VMEM((pieces, 2, piece, REACH * BLOCK), bf16),
                pltpu.VMEM((pieces, piece, width), bf16),
                pltpu.VMEM((XZERO + 1, piece, BLOCK), bf16),
                pltpu.VMEM((SLOTS * HSTEP, piece, BLOCK), bf16),
                pltpu.VMEM(bias.shape, f32),
                pltpu.VMEM(bias.shape, f32),
                pltpu.SMEM(offset.shape, i32),
                pltpu.SMEM(offset.shape, i32),
                pltpu.SMEM(block_count.shape, i32),
                pltpu.SMEM(block_count.shape, i32),
                pltpu.SMEM((EDGE * KMAX,), i32),
                pltpu.SMEM((ROWS * KMAX,), i32),
                pltpu.VMEM((8, SAMPLES), f32),
                dma((3,)), dma((6,)), dma((6,)), dma((2,)), dma((2,)),
                dma((pieces, 2)), dma((pieces, 2)), dma((pieces, 2)), dma((pieces, 2)),
                dma((pieces, 2)), dma((pieces, 2)), dma((pieces, 2)), dma((pieces,)),
            ],
            compiler_params=pltpu.CompilerParams(
                collective_id=0, has_side_effects=True, vmem_limit_bytes=56 << 20
            ),
        )(
            samples, batch_of, weights, bias, offset, block_count,
            bias, offset, block_count,
        )
        return result.reshape(1, NMB, S, width)

    return jax.shard_map(
        on_device,
        mesh=mesh,
        in_specs=(
            P(None, "neuron"),
            P(),
            P("segment", "neuron", None, None, None),
            P("segment", "neuron", None),
            P("segment", "neuron"),
            P("segment", "neuron"),
        ),
        out_specs=P("segment", None, None, "neuron"),
        check_vma=False,
    )
```

```python
import functools

import jax
import jax.numpy as jnp
from jax import lax
from jax.experimental import pallas as pl
from jax.experimental.pallas import tpu as pltpu
from jax.sharding import PartitionSpec as P

MESH = pl.DeviceIdType.MESH
BLOCK = 128
KMAX = 5
REACH = 4
S = 128
NMB = 3
ROWS = 16
WIDE = 2 * REACH
EDGE = ROWS + 2 * REACH
XZERO = ROWS + 2 * WIDE
HZERO = EDGE
HSTEP = EDGE + 1
HALF = ROWS // 2
SAMPLES = S * NMB
AHEAD = 2
LAG = 2
SLOTS = LAG + 1


def kernel(
    segments, neurons, piece,
    samples, batch, weights, bias_any, offset_any, count_any, bias, offset, count,
    out,
    wa, wb, raw, main, halo, mid, mid_out, result, x, h, bias_l, bias_r,
    off_l, off_r, cnt_l, cnt_r, ia, ib, pos,
    load_sem, info_send, info_recv, w_send, w_recv,
    main_send, main_recv, halo_send, halo_recv, fwd_send, mid_send, mid_recv, out_sem,
):
    pieces = SAMPLES // piece
    s = lax.axis_index("segment")
    n = lax.axis_index("neuron")
    left = jnp.maximum(n - 1, 0)
    right = jnp.minimum(n + 1, neurons - 1)
    there = (n > 0, n < neurons - 1)
    odd = lax.rem(s, 2)
    first = s == 0
    even = odd == 0
    last = s == segments - 1
    pair = s + 1 - 2 * odd
    crossing = jnp.logical_not(first) & jnp.logical_not(last)
    other = jnp.clip(s - 1 + 2 * odd, 0, segments - 1)

    def remote(src, dst, send, recv, device):
        return pltpu.make_async_remote_copy(
            src_ref=src, dst_ref=dst, send_sem=send, recv_sem=recv,
            device_id=device, device_id_type=MESH,
        )

    load_a = pltpu.make_async_copy(weights.at[0], wa.at[pl.ds(REACH, ROWS)], load_sem.at[0])
    load_b = pltpu.make_async_copy(weights.at[1], wb, load_sem.at[1])
    load_s = pltpu.make_async_copy(samples, raw, load_sem.at[2])
    pl.when(first)(load_s.start)
    load_a.start()
    load_b.start()

    barrier = pltpu.get_barrier_semaphore()

    def greet(device):
        pl.semaphore_signal(barrier, inc=1, device_id=device, device_id_type=MESH)

    for side, neighbour in enumerate((left, right)):

        @pl.when(there[side])
        def _():
            greet((s, neighbour))
            greet((pair, neighbour))

    greet((pair, n))
    pl.when(crossing)(lambda: greet((other, n)))

    blank = jnp.zeros((piece, BLOCK), jnp.bfloat16)
    x[XZERO] = blank
    for slot in range(SLOTS):
        h[slot * HSTEP + HZERO] = blank
    for side, (b_side, a_row) in enumerate(((bias_l, 0), (bias_r, REACH + ROWS))):

        @pl.when(jnp.logical_not(there[side]))
        def _():
            for j in range(WIDE):
                x[side * (WIDE + ROWS) + j] = blank
            for slot in range(SLOTS):
                for j in range(REACH):
                    h[slot * HSTEP + a_row + j] = blank
            b_side[...] = jnp.zeros(b_side.shape, jnp.float32)
            for j in range(REACH):
                wa[a_row + j] = jnp.zeros(wa.shape[1:], jnp.bfloat16)
                for k in range(KMAX):
                    ia[(a_row + j) * KMAX + k] = XZERO

    @pl.when(first)
    def _():
        lanes = lax.broadcasted_iota(jnp.int32, (8, SAMPLES), 0)
        hot = jnp.where(jnp.broadcast_to(batch[...].reshape(1, SAMPLES), (8, SAMPLES)) == lanes, 1.0, 0.0)
        before = jnp.where(
            lax.broadcasted_iota(jnp.int32, (SAMPLES, SAMPLES), 0)
            < lax.broadcasted_iota(jnp.int32, (SAMPLES, SAMPLES), 1),
            1.0, 0.0,
        ).astype(jnp.bfloat16)
        rank = jnp.dot(hot.astype(jnp.bfloat16), before, preferred_element_type=jnp.float32)
        place = hot * (rank + lanes.astype(jnp.float32) * float(S))
        pos[...] = jnp.broadcast_to(jnp.sum(place, axis=0, keepdims=True), (8, SAMPLES))

    greeted = 1 + crossing.astype(jnp.int32)
    for side in range(2):
        greeted = greeted + 2 * there[side].astype(jnp.int32)
    pl.semaphore_wait(barrier, greeted)

    info = [
        remote(offset_any, off_r, info_send.at[0], info_recv.at[0], (s, left)),
        remote(offset_any, off_l, info_send.at[1], info_recv.at[1], (s, right)),
        remote(count_any, cnt_r, info_send.at[2], info_recv.at[2], (s, left)),
        remote(count_any, cnt_l, info_send.at[3], info_recv.at[3], (s, right)),
        remote(bias_any, bias_r, info_send.at[4], info_recv.at[4], (s, left)),
        remote(bias_any, bias_l, info_send.at[5], info_recv.at[5], (s, right)),
    ]
    rows_of_neighbours = [
        remote(
            weights.at[0, pl.ds(0, REACH)], wa.at[pl.ds(REACH + ROWS, REACH)],
            w_send.at[0], w_recv.at[0], (s, left),
        ),
        remote(
            weights.at[0, pl.ds(ROWS - REACH, REACH)], wa.at[pl.ds(0, REACH)],
            w_send.at[1], w_recv.at[1], (s, right),
        ),
    ]

    for side in range(2):

        @pl.when(jnp.logical_not(first) & there[side])
        def _():
            for copy in info[side::2]:
                copy.start()
            rows_of_neighbours[side].start()

    def main_copy(p, half, device):
        cols = pl.ds(half * HALF * BLOCK, HALF * BLOCK)
        return remote(
            result.at[p, :, cols], main.at[p, :, cols],
            main_send.at[p, half], main_recv.at[p, half], device,
        )

    def halo_copy(p, half, device):
        cols = pl.ds(half * HALF * BLOCK, HALF * BLOCK)
        return remote(
            result.at[p, :, cols], halo.at[p, 1 - half],
            halo_send.at[p, half], halo_recv.at[p, 1 - half], device,
        )

    def fwd_copy(p, half, device):
        cols = pl.ds(half * HALF * BLOCK, HALF * BLOCK)
        return remote(
            main.at[p, :, cols], halo.at[p, 1 - half],
            fwd_send.at[p, half], halo_recv.at[p, 1 - half], device,
        )

    def narrow_copy(p, half, device):
        width = REACH * BLOCK
        src = pl.ds(half * (ROWS - REACH) * BLOCK, width)
        dst = pl.ds(half * REACH * BLOCK, width)
        return remote(
            main.at[p, :, src], halo.at[p, 1 - half, :, dst],
            fwd_send.at[p, half], halo_recv.at[p, 1 - half], device,
        )

    def mid_copy(p, half, device):
        return remote(
            mid_out.at[p, half], mid.at[p, 1 - half],
            mid_send.at[p, half], mid_recv.at[p, 1 - half], device,
        )

    sides = ((0, (s, left)), (1, (s, right)))
    pair_sides = ((0, (pair, left)), (1, (pair, right)))

    def prepare(p):
        @pl.when(first)
        def _():
            want = lax.broadcasted_iota(jnp.int32, (piece, SAMPLES), 0) + p * piece
            pick = jnp.where(
                jnp.broadcast_to(pos[0:1, :], (piece, SAMPLES)) == want.astype(jnp.float32),
                1.0, 0.0,
            ).astype(jnp.bfloat16)
            for c in range(0, ROWS * BLOCK, 2 * BLOCK):
                main[p, :, c : c + 2 * BLOCK] = jnp.dot(
                    pick, raw[:, c : c + 2 * BLOCK], preferred_element_type=jnp.float32
                ).astype(jnp.bfloat16)
            for half, device in sides:
                pl.when(there[half])(narrow_copy(p, half, device).start)

        @pl.when(jnp.logical_not(first))
        def _():
            for half, device in sides:
                main_copy(p, half, (s, n)).wait_recv()
                pl.when(there[half])(fwd_copy(p, half, device).start)

    def first_rows(rows, slot, keep):
        for a in rows:
            taken = jnp.concatenate([x[ia[a * KMAX + k]] for k in range(KMAX)], axis=1)
            y = jnp.dot(
                taken, wa[a].reshape(KMAX * BLOCK, BLOCK), preferred_element_type=jnp.float32
            )
            j = a - REACH
            if j < 0:
                b = bias_l[0:1, (j + ROWS) * BLOCK : (j + ROWS + 1) * BLOCK]
            elif j < ROWS:
                b = bias[0:1, j * BLOCK : (j + 1) * BLOCK]
            else:
                b = bias_r[0:1, (j - ROWS) * BLOCK : (j - ROWS + 1) * BLOCK]
            y = jnp.maximum(y + b, 0.0).astype(jnp.bfloat16)
            h[slot * HSTEP + a] = y
            if keep is not None:
                keep(j, y)

    def second_rows(rows, slot, p):
        for j in rows:
            taken = jnp.concatenate(
                [h[slot * HSTEP + ib[j * KMAX + k]] for k in range(KMAX)], axis=1
            )
            y = jnp.dot(
                taken, wb[j].reshape(KMAX * BLOCK, BLOCK), preferred_element_type=jnp.float32
            )
            b = bias[1:2, j * BLOCK : (j + 1) * BLOCK]
            result[p, :, j * BLOCK : (j + 1) * BLOCK] = jnp.maximum(y + b, 0.0).astype(jnp.bfloat16)

    def stage_a(p):
        slot = lax.rem(p, SLOTS)

        @pl.when(jnp.logical_not(even))
        def _():
            for half, _ in sides:
                main_copy(p, half, (pair, n)).wait_recv()

        for j in range(ROWS):
            x[WIDE + j] = main[p, :, j * BLOCK : (j + 1) * BLOCK]
        first_rows(range(2 * REACH, EDGE - 2 * REACH), slot, None)

        @pl.when(first)
        def _():
            @pl.when(there[0])
            def _():
                narrow_copy(p, 1, (s, left)).wait_recv()
                for j in range(REACH, WIDE):
                    x[j] = halo[p, 0, :, j * BLOCK : (j + 1) * BLOCK]

            @pl.when(there[1])
            def _():
                narrow_copy(p, 0, (s, right)).wait_recv()
                for j in range(REACH):
                    x[WIDE + ROWS + j] = halo[p, 1, :, j * BLOCK : (j + 1) * BLOCK]

            def keep(j, y):
                half = 0 if j < REACH else 1
                c = (j - half * (ROWS - REACH)) * BLOCK
                mid_out[p, half, :, c : c + BLOCK] = y

            first_rows(range(REACH, 2 * REACH), slot, keep)
            first_rows(range(EDGE - 2 * REACH, EDGE - REACH), slot, keep)
            for half, device in sides:
                pl.when(there[half])(mid_copy(p, half, device).start)

        @pl.when(jnp.logical_not(first))
        def _():
            for side in range(2):

                @pl.when(there[side])
                def _():
                    fwd_copy(p, 1 - side, sides[side][1]).wait_recv()
                    for j in range(WIDE):
                        x[side * (WIDE + ROWS) + j] = halo[p, side, :, j * BLOCK : (j + 1) * BLOCK]
            first_rows(range(2 * REACH), slot, None)
            first_rows(range(EDGE - 2 * REACH, EDGE), slot, None)

    def stage_b(p):
        slot = lax.rem(p, SLOTS)

        @pl.when(first)
        def _():
            for side in range(2):

                @pl.when(there[side])
                def _():
                    mid_copy(p, 1 - side, sides[side][1]).wait_recv()
                    for j in range(REACH):
                        h[slot * HSTEP + side * (REACH + ROWS) + j] = mid[
                            p, side, :, j * BLOCK : (j + 1) * BLOCK
                        ]

        for half in range(2):
            second_rows(range(half * HALF, (half + 1) * HALF), slot, p)

            @pl.when(even)
            def _():
                pl.when(there[half])(halo_copy(p, half, pair_sides[half][1]).start)
                main_copy(p, half, (pair, n)).start()

            @pl.when(jnp.logical_not(even) & jnp.logical_not(last))
            def _():
                main_copy(p, half, (other, n)).start()

        out_copy(p).start()

    def out_copy(p):
        return pltpu.make_async_copy(
            result.at[p], out.at[pl.ds(p * piece, piece), :], out_sem.at[p]
        )

    def fill(table, entry, off_ref, cnt_ref, layer, row, j, base, zero):
        used = cnt_ref[layer, row]
        for k in range(KMAX):
            off = off_ref[k, layer, row]
            place = n * ROWS + j + off
            live = (k < used) & (place >= 0) & (place < neurons * ROWS)
            table[entry * KMAX + k] = jnp.where(live, base + j + off, zero)

    def own(r, carry):
        fill(ia, r + REACH, offset, count, 0, r, r, WIDE, XZERO)
        fill(ib, r, offset, count, 1, r, r, REACH, HZERO)
        return carry

    @pl.when(first)
    def _():
        load_s.wait()
        for p in range(AHEAD):
            prepare(p)

    lax.fori_loop(0, ROWS, own, 0)

    @pl.when(jnp.logical_not(first))
    def _():
        for side, (off_side, cnt_side, row) in enumerate(
            ((off_l, cnt_l, ROWS - REACH), (off_r, cnt_r, 0))
        ):

            @pl.when(there[side])
            def _():
                for copy in info[1 - side :: 2]:
                    copy.wait_recv()

                def side_row(r, carry):
                    j = r - REACH + side * (REACH + ROWS)
                    fill(ia, j + REACH, off_side, cnt_side, 0, row + r, j, WIDE, XZERO)
                    return carry

                lax.fori_loop(0, REACH, side_row, 0)
                rows_of_neighbours[1 - side].wait_recv()

    load_a.wait()
    load_b.wait()

    @pl.when(even & jnp.logical_not(first))
    def _():
        for p in range(AHEAD):
            prepare(p)

    def step(q, carry):
        @pl.when(q < pieces)
        def _():
            pl.when(even & (q + AHEAD < pieces))(lambda: prepare(q + AHEAD))
            stage_a(q)

        p = q - jnp.where(first, LAG, 0)
        pl.when((p >= 0) & (p < pieces))(lambda: stage_b(p))
        return carry

    lax.fori_loop(0, pieces + LAG, step, 0)

    for side in range(2):

        @pl.when(jnp.logical_not(first) & there[side])
        def _():
            for copy in info[side::2]:
                copy.wait_send()
            rows_of_neighbours[side].wait_send()

    def drain(p, carry):
        out_copy(p).wait()
        for half in range(2):
            pl.when(jnp.logical_not(last))(lambda: main_copy(p, half, (pair, n)).wait_send())

            @pl.when(there[half])
            def _():
                pl.when(even)(lambda: halo_copy(p, half, pair_sides[half][1]).wait_send())
                pl.when(first)(lambda: narrow_copy(p, half, sides[half][1]).wait_send())
                pl.when(first)(lambda: mid_copy(p, half, sides[half][1]).wait_send())
                pl.when(even & jnp.logical_not(first))(
                    lambda: fwd_copy(p, half, sides[half][1]).wait_send()
                )

        return carry

    lax.fori_loop(0, pieces, drain, 0)


def solution(mesh):
    segments, neurons = mesh.shape["segment"], mesh.shape["neuron"]
    piece = 48
    pieces = SAMPLES // piece
    width = ROWS * BLOCK
    bf16, f32, i32 = jnp.bfloat16, jnp.float32, jnp.int32

    def on_device(samples, batch_of, weights, block_offset, block_count, bias):
        dma = pltpu.SemaphoreType.DMA
        vmem = pl.BlockSpec(memory_space=pltpu.VMEM)
        smem = pl.BlockSpec(memory_space=pltpu.SMEM)
        hbm = pl.BlockSpec(memory_space=pl.ANY)
        offset = block_offset.transpose(2, 0, 1)
        result = pl.pallas_call(
            functools.partial(kernel, segments, neurons, piece),
            out_shape=jax.ShapeDtypeStruct((SAMPLES, width), bf16),
            in_specs=[hbm, vmem, hbm, hbm, hbm, hbm, vmem, smem, smem],
            out_specs=hbm,
            scratch_shapes=[
                pltpu.VMEM((EDGE, KMAX, BLOCK, BLOCK), bf16),
                pltpu.VMEM((ROWS, KMAX, BLOCK, BLOCK), bf16),
                pltpu.VMEM((SAMPLES, width), bf16),
                pltpu.VMEM((pieces, piece, width), bf16),
                pltpu.VMEM((pieces, 2, piece, WIDE * BLOCK), bf16),
                pltpu.VMEM((pieces, 2, piece, REACH * BLOCK), bf16),
                pltpu.VMEM((pieces, 2, piece, REACH * BLOCK), bf16),
                pltpu.VMEM((pieces, piece, width), bf16),
                pltpu.VMEM((XZERO + 1, piece, BLOCK), bf16),
                pltpu.VMEM((SLOTS * HSTEP, piece, BLOCK), bf16),
                pltpu.VMEM(bias.shape, f32),
                pltpu.VMEM(bias.shape, f32),
                pltpu.SMEM(offset.shape, i32),
                pltpu.SMEM(offset.shape, i32),
                pltpu.SMEM(block_count.shape, i32),
                pltpu.SMEM(block_count.shape, i32),
                pltpu.SMEM((EDGE * KMAX,), i32),
                pltpu.SMEM((ROWS * KMAX,), i32),
                pltpu.VMEM((8, SAMPLES), f32),
                dma((3,)), dma((6,)), dma((6,)), dma((2,)), dma((2,)),
                dma((pieces, 2)), dma((pieces, 2)), dma((pieces, 2)), dma((pieces, 2)),
                dma((pieces, 2)), dma((pieces, 2)), dma((pieces, 2)), dma((pieces,)),
            ],
            compiler_params=pltpu.CompilerParams(
                collective_id=0, has_side_effects=True, vmem_limit_bytes=56 << 20
            ),
        )(
            samples, batch_of, weights, bias, offset, block_count,
            bias, offset, block_count,
        )
        return result.reshape(1, NMB, S, width)

    return jax.shard_map(
        on_device,
        mesh=mesh,
        in_specs=(
            P(None, "neuron"),
            P(),
            P("segment", "neuron", None, None, None),
            P("segment", "neuron", None),
            P("segment", "neuron"),
            P("segment", "neuron"),
        ),
        out_specs=P("segment", None, None, "neuron"),
        check_vma=False,
    )
```

```python
import functools

import jax
import jax.numpy as jnp
from jax import lax
from jax.experimental import pallas as pl
from jax.experimental.pallas import tpu as pltpu
from jax.sharding import PartitionSpec as P

MESH = pl.DeviceIdType.MESH
BLOCK = 128
KMAX = 5
REACH = 4
S = 128
NMB = 3
ROWS = 16
WIDE = 2 * REACH
EDGE = ROWS + 2 * REACH
XZERO = ROWS + 2 * WIDE
HZERO = EDGE
HSTEP = EDGE + 1
HALF = ROWS // 2
SAMPLES = S * NMB
AHEAD = 2
LAG = 2
SLOTS = LAG + 1


def kernel(
    segments, neurons, piece,
    samples, batch, weights, bias_any, offset_any, count_any, bias, offset, count,
    out,
    wa, wb, raw, main, halo, mid, mid_out, result, x, h, bias_l, bias_r,
    off_l, off_r, cnt_l, cnt_r, ia, ib, pos,
    load_sem, info_send, info_recv, w_send, w_recv,
    main_send, main_recv, halo_send, halo_recv, fwd_send, mid_send, mid_recv, outer_send, outer_recv, out_sem,
):
    pieces = SAMPLES // piece
    s = lax.axis_index("segment")
    n = lax.axis_index("neuron")
    left = jnp.maximum(n - 1, 0)
    right = jnp.minimum(n + 1, neurons - 1)
    there = (n > 0, n < neurons - 1)
    odd = lax.rem(s, 2)
    first = s == 0
    even = odd == 0
    last = s == segments - 1
    pair = s + 1 - 2 * odd
    crossing = jnp.logical_not(first) & jnp.logical_not(last)
    other = jnp.clip(s - 1 + 2 * odd, 0, segments - 1)

    def remote(src, dst, send, recv, device):
        return pltpu.make_async_remote_copy(
            src_ref=src, dst_ref=dst, send_sem=send, recv_sem=recv,
            device_id=device, device_id_type=MESH,
        )

    load_a = pltpu.make_async_copy(weights.at[0], wa.at[pl.ds(REACH, ROWS)], load_sem.at[0])
    load_b = pltpu.make_async_copy(weights.at[1], wb, load_sem.at[1])
    load_s = pltpu.make_async_copy(samples, raw, load_sem.at[2])
    pl.when(first)(load_s.start)
    load_a.start()
    load_b.start()

    barrier = pltpu.get_barrier_semaphore()

    def greet(device):
        pl.semaphore_signal(barrier, inc=1, device_id=device, device_id_type=MESH)

    for side, neighbour in enumerate((left, right)):

        @pl.when(there[side])
        def _():
            greet((s, neighbour))
            greet((pair, neighbour))

    greet((pair, n))
    pl.when(crossing)(lambda: greet((other, n)))

    blank = jnp.zeros((piece, BLOCK), jnp.bfloat16)
    x[XZERO] = blank
    for slot in range(SLOTS):
        h[slot * HSTEP + HZERO] = blank
    for side, (b_side, a_row) in enumerate(((bias_l, 0), (bias_r, REACH + ROWS))):

        @pl.when(jnp.logical_not(there[side]))
        def _():
            for j in range(WIDE):
                x[side * (WIDE + ROWS) + j] = blank
            for slot in range(SLOTS):
                for j in range(REACH):
                    h[slot * HSTEP + a_row + j] = blank
            b_side[...] = jnp.zeros(b_side.shape, jnp.float32)
            for j in range(REACH):
                wa[a_row + j] = jnp.zeros(wa.shape[1:], jnp.bfloat16)
                for k in range(KMAX):
                    ia[(a_row + j) * KMAX + k] = XZERO

    @pl.when(first)
    def _():
        lanes = lax.broadcasted_iota(jnp.int32, (8, SAMPLES), 0)
        hot = jnp.where(jnp.broadcast_to(batch[...].reshape(1, SAMPLES), (8, SAMPLES)) == lanes, 1.0, 0.0)
        before = jnp.where(
            lax.broadcasted_iota(jnp.int32, (SAMPLES, SAMPLES), 0)
            < lax.broadcasted_iota(jnp.int32, (SAMPLES, SAMPLES), 1),
            1.0, 0.0,
        ).astype(jnp.bfloat16)
        rank = jnp.dot(hot.astype(jnp.bfloat16), before, preferred_element_type=jnp.float32)
        place = hot * (rank + lanes.astype(jnp.float32) * float(S))
        pos[...] = jnp.broadcast_to(jnp.sum(place, axis=0, keepdims=True), (8, SAMPLES))

    greeted = 1 + crossing.astype(jnp.int32)
    for side in range(2):
        greeted = greeted + 2 * there[side].astype(jnp.int32)
    pl.semaphore_wait(barrier, greeted)

    info = [
        remote(offset_any, off_r, info_send.at[0], info_recv.at[0], (s, left)),
        remote(offset_any, off_l, info_send.at[1], info_recv.at[1], (s, right)),
        remote(count_any, cnt_r, info_send.at[2], info_recv.at[2], (s, left)),
        remote(count_any, cnt_l, info_send.at[3], info_recv.at[3], (s, right)),
        remote(bias_any, bias_r, info_send.at[4], info_recv.at[4], (s, left)),
        remote(bias_any, bias_l, info_send.at[5], info_recv.at[5], (s, right)),
    ]
    rows_of_neighbours = [
        remote(
            weights.at[0, pl.ds(0, REACH)], wa.at[pl.ds(REACH + ROWS, REACH)],
            w_send.at[0], w_recv.at[0], (s, left),
        ),
        remote(
            weights.at[0, pl.ds(ROWS - REACH, REACH)], wa.at[pl.ds(0, REACH)],
            w_send.at[1], w_recv.at[1], (s, right),
        ),
    ]

    for side in range(2):

        @pl.when(jnp.logical_not(first) & there[side])
        def _():
            for copy in info[side::2]:
                copy.start()
            rows_of_neighbours[side].start()

    def main_copy(p, half, device):
        cols = pl.ds(half * HALF * BLOCK, HALF * BLOCK)
        return remote(
            result.at[p, :, cols], main.at[p, :, cols],
            main_send.at[p, half], main_recv.at[p, half], device,
        )

    def halo_copy(p, half, device, outer):
        src = half * (ROWS - REACH) if outer else REACH + half * REACH
        send, recv = (outer_send, outer_recv) if outer else (halo_send, halo_recv)
        return remote(
            result.at[p, :, pl.ds(src * BLOCK, REACH * BLOCK)],
            halo.at[p, 1 - half, :, pl.ds((src - half * HALF) * BLOCK, REACH * BLOCK)],
            send.at[p, half], recv.at[p, 1 - half], device,
        )

    def fwd_copy(p, half, device):
        cols = pl.ds(half * HALF * BLOCK, HALF * BLOCK)
        return remote(
            main.at[p, :, cols], halo.at[p, 1 - half],
            fwd_send.at[p, half], halo_recv.at[p, 1 - half], device,
        )

    def narrow_copy(p, half, device):
        width = REACH * BLOCK
        src = pl.ds(half * (ROWS - REACH) * BLOCK, width)
        dst = pl.ds(half * REACH * BLOCK, width)
        return remote(
            main.at[p, :, src], halo.at[p, 1 - half, :, dst],
            fwd_send.at[p, half], halo_recv.at[p, 1 - half], device,
        )

    def mid_copy(p, half, device):
        return remote(
            mid_out.at[p, half], mid.at[p, 1 - half],
            mid_send.at[p, half], mid_recv.at[p, 1 - half], device,
        )

    sides = ((0, (s, left)), (1, (s, right)))
    pair_sides = ((0, (pair, left)), (1, (pair, right)))

    def prepare(p):
        @pl.when(first)
        def _():
            want = lax.broadcasted_iota(jnp.int32, (piece, SAMPLES), 0) + p * piece
            pick = jnp.where(
                jnp.broadcast_to(pos[0:1, :], (piece, SAMPLES)) == want.astype(jnp.float32),
                1.0, 0.0,
            ).astype(jnp.bfloat16)
            for c in range(0, ROWS * BLOCK, 2 * BLOCK):
                main[p, :, c : c + 2 * BLOCK] = jnp.dot(
                    pick, raw[:, c : c + 2 * BLOCK], preferred_element_type=jnp.float32
                ).astype(jnp.bfloat16)
            for half, device in sides:
                pl.when(there[half])(narrow_copy(p, half, device).start)

        @pl.when(jnp.logical_not(first))
        def _():
            for half, device in sides:
                main_copy(p, half, (s, n)).wait_recv()
                pl.when(there[half])(fwd_copy(p, half, device).start)

    def first_rows(rows, slot, keep):
        for a in rows:
            taken = jnp.concatenate([x[ia[a * KMAX + k]] for k in range(KMAX)], axis=1)
            y = jnp.dot(
                taken, wa[a].reshape(KMAX * BLOCK, BLOCK), preferred_element_type=jnp.float32
            )
            j = a - REACH
            if j < 0:
                b = bias_l[0:1, (j + ROWS) * BLOCK : (j + ROWS + 1) * BLOCK]
            elif j < ROWS:
                b = bias[0:1, j * BLOCK : (j + 1) * BLOCK]
            else:
                b = bias_r[0:1, (j - ROWS) * BLOCK : (j - ROWS + 1) * BLOCK]
            y = jnp.maximum(y + b, 0.0).astype(jnp.bfloat16)
            h[slot * HSTEP + a] = y
            if keep is not None:
                keep(j, y)

    def second_rows(rows, slot, p):
        for j in rows:
            taken = jnp.concatenate(
                [h[slot * HSTEP + ib[j * KMAX + k]] for k in range(KMAX)], axis=1
            )
            y = jnp.dot(
                taken, wb[j].reshape(KMAX * BLOCK, BLOCK), preferred_element_type=jnp.float32
            )
            b = bias[1:2, j * BLOCK : (j + 1) * BLOCK]
            result[p, :, j * BLOCK : (j + 1) * BLOCK] = jnp.maximum(y + b, 0.0).astype(jnp.bfloat16)

    def stage_a(p):
        slot = lax.rem(p, SLOTS)

        @pl.when(jnp.logical_not(even))
        def _():
            for half, _ in sides:
                main_copy(p, half, (pair, n)).wait_recv()

        for j in range(ROWS):
            x[WIDE + j] = main[p, :, j * BLOCK : (j + 1) * BLOCK]
        first_rows(range(2 * REACH, EDGE - 2 * REACH), slot, None)

        @pl.when(first)
        def _():
            @pl.when(there[0])
            def _():
                narrow_copy(p, 1, (s, left)).wait_recv()
                for j in range(REACH, WIDE):
                    x[j] = halo[p, 0, :, j * BLOCK : (j + 1) * BLOCK]

            @pl.when(there[1])
            def _():
                narrow_copy(p, 0, (s, right)).wait_recv()
                for j in range(REACH):
                    x[WIDE + ROWS + j] = halo[p, 1, :, j * BLOCK : (j + 1) * BLOCK]

            def keep(j, y):
                half = 0 if j < REACH else 1
                c = (j - half * (ROWS - REACH)) * BLOCK
                mid_out[p, half, :, c : c + BLOCK] = y

            first_rows(range(REACH, 2 * REACH), slot, keep)
            first_rows(range(EDGE - 2 * REACH, EDGE - REACH), slot, keep)
            for half, device in sides:
                pl.when(there[half])(mid_copy(p, half, device).start)

        @pl.when(jnp.logical_not(first))
        def _():
            for side in range(2):

                @pl.when(there[side])
                def _():
                    pl.when(even)(fwd_copy(p, 1 - side, sides[side][1]).wait_recv)

                    @pl.when(jnp.logical_not(even))
                    def _():
                        for outer in (True, False):
                            halo_copy(p, 1 - side, pair_sides[side][1], outer).wait_recv()

                    for j in range(WIDE):
                        x[side * (WIDE + ROWS) + j] = halo[p, side, :, j * BLOCK : (j + 1) * BLOCK]
            first_rows(range(2 * REACH), slot, None)
            first_rows(range(EDGE - 2 * REACH, EDGE), slot, None)

    def stage_b(p):
        slot = lax.rem(p, SLOTS)

        @pl.when(first)
        def _():
            for side in range(2):

                @pl.when(there[side])
                def _():
                    mid_copy(p, 1 - side, sides[side][1]).wait_recv()
                    for j in range(REACH):
                        h[slot * HSTEP + side * (REACH + ROWS) + j] = mid[
                            p, side, :, j * BLOCK : (j + 1) * BLOCK
                        ]

        @pl.when(even)
        def _():
            ends = [*range(REACH), *range(ROWS - REACH, ROWS)]
            for rows, outer in ((ends, True), (range(REACH, ROWS - REACH), False)):
                second_rows(rows, slot, p)
                for half, device in pair_sides:
                    pl.when(there[half])(halo_copy(p, half, device, outer).start)
            for half in range(2):
                main_copy(p, half, (pair, n)).start()

        @pl.when(jnp.logical_not(even))
        def _():
            for half in range(2):
                second_rows(range(half * HALF, (half + 1) * HALF), slot, p)
                pl.when(jnp.logical_not(last))(main_copy(p, half, (other, n)).start)

        out_copy(p).start()

    def out_copy(p):
        return pltpu.make_async_copy(
            result.at[p], out.at[pl.ds(p * piece, piece), :], out_sem.at[p]
        )

    def fill(table, entry, off_ref, cnt_ref, layer, row, j, base, zero):
        used = cnt_ref[layer, row]
        for k in range(KMAX):
            off = off_ref[k, layer, row]
            place = n * ROWS + j + off
            live = (k < used) & (place >= 0) & (place < neurons * ROWS)
            table[entry * KMAX + k] = jnp.where(live, base + j + off, zero)

    def own(r, carry):
        fill(ia, r + REACH, offset, count, 0, r, r, WIDE, XZERO)
        fill(ib, r, offset, count, 1, r, r, REACH, HZERO)
        return carry

    @pl.when(first)
    def _():
        load_s.wait()
        for p in range(AHEAD):
            prepare(p)

    lax.fori_loop(0, ROWS, own, 0)

    @pl.when(jnp.logical_not(first))
    def _():
        for side, (off_side, cnt_side, row) in enumerate(
            ((off_l, cnt_l, ROWS - REACH), (off_r, cnt_r, 0))
        ):

            @pl.when(there[side])
            def _():
                for copy in info[1 - side :: 2]:
                    copy.wait_recv()

                def side_row(r, carry):
                    j = r - REACH + side * (REACH + ROWS)
                    fill(ia, j + REACH, off_side, cnt_side, 0, row + r, j, WIDE, XZERO)
                    return carry

                lax.fori_loop(0, REACH, side_row, 0)
                rows_of_neighbours[1 - side].wait_recv()

    load_a.wait()
    load_b.wait()

    @pl.when(even & jnp.logical_not(first))
    def _():
        for p in range(AHEAD):
            prepare(p)

    def step(q, carry):
        @pl.when(q < pieces)
        def _():
            pl.when(even & (q + AHEAD < pieces))(lambda: prepare(q + AHEAD))
            stage_a(q)

        p = q - jnp.where(first, LAG, 0)
        pl.when((p >= 0) & (p < pieces))(lambda: stage_b(p))
        return carry

    lax.fori_loop(0, pieces + LAG, step, 0)

    for side in range(2):

        @pl.when(jnp.logical_not(first) & there[side])
        def _():
            for copy in info[side::2]:
                copy.wait_send()
            rows_of_neighbours[side].wait_send()

    def drain(p, carry):
        out_copy(p).wait()
        for half in range(2):
            pl.when(jnp.logical_not(last))(lambda: main_copy(p, half, (pair, n)).wait_send())

            @pl.when(there[half])
            def _():
                for outer in (True, False):
                    pl.when(even)(
                        lambda: halo_copy(p, half, pair_sides[half][1], outer).wait_send()
                    )
                pl.when(first)(lambda: narrow_copy(p, half, sides[half][1]).wait_send())
                pl.when(first)(lambda: mid_copy(p, half, sides[half][1]).wait_send())
                pl.when(even & jnp.logical_not(first))(
                    lambda: fwd_copy(p, half, sides[half][1]).wait_send()
                )

        return carry

    lax.fori_loop(0, pieces, drain, 0)


def solution(mesh):
    segments, neurons = mesh.shape["segment"], mesh.shape["neuron"]
    piece = 48
    pieces = SAMPLES // piece
    width = ROWS * BLOCK
    bf16, f32, i32 = jnp.bfloat16, jnp.float32, jnp.int32

    def on_device(samples, batch_of, weights, block_offset, block_count, bias):
        dma = pltpu.SemaphoreType.DMA
        vmem = pl.BlockSpec(memory_space=pltpu.VMEM)
        smem = pl.BlockSpec(memory_space=pltpu.SMEM)
        hbm = pl.BlockSpec(memory_space=pl.ANY)
        offset = block_offset.transpose(2, 0, 1)
        result = pl.pallas_call(
            functools.partial(kernel, segments, neurons, piece),
            out_shape=jax.ShapeDtypeStruct((SAMPLES, width), bf16),
            in_specs=[hbm, vmem, hbm, hbm, hbm, hbm, vmem, smem, smem],
            out_specs=hbm,
            scratch_shapes=[
                pltpu.VMEM((EDGE, KMAX, BLOCK, BLOCK), bf16),
                pltpu.VMEM((ROWS, KMAX, BLOCK, BLOCK), bf16),
                pltpu.VMEM((SAMPLES, width), bf16),
                pltpu.VMEM((pieces, piece, width), bf16),
                pltpu.VMEM((pieces, 2, piece, WIDE * BLOCK), bf16),
                pltpu.VMEM((pieces, 2, piece, REACH * BLOCK), bf16),
                pltpu.VMEM((pieces, 2, piece, REACH * BLOCK), bf16),
                pltpu.VMEM((pieces, piece, width), bf16),
                pltpu.VMEM((XZERO + 1, piece, BLOCK), bf16),
                pltpu.VMEM((SLOTS * HSTEP, piece, BLOCK), bf16),
                pltpu.VMEM(bias.shape, f32),
                pltpu.VMEM(bias.shape, f32),
                pltpu.SMEM(offset.shape, i32),
                pltpu.SMEM(offset.shape, i32),
                pltpu.SMEM(block_count.shape, i32),
                pltpu.SMEM(block_count.shape, i32),
                pltpu.SMEM((EDGE * KMAX,), i32),
                pltpu.SMEM((ROWS * KMAX,), i32),
                pltpu.VMEM((8, SAMPLES), f32),
                dma((3,)), dma((6,)), dma((6,)), dma((2,)), dma((2,)),
                dma((pieces, 2)), dma((pieces, 2)), dma((pieces, 2)), dma((pieces, 2)),
                dma((pieces, 2)), dma((pieces, 2)), dma((pieces, 2)), dma((pieces, 2)), dma((pieces, 2)),
                dma((pieces,)),
            ],
            compiler_params=pltpu.CompilerParams(
                collective_id=0, has_side_effects=True, vmem_limit_bytes=56 << 20
            ),
        )(
            samples, batch_of, weights, bias, offset, block_count,
            bias, offset, block_count,
        )
        return result.reshape(1, NMB, S, width)

    return jax.shard_map(
        on_device,
        mesh=mesh,
        in_specs=(
            P(None, "neuron"),
            P(),
            P("segment", "neuron", None, None, None),
            P("segment", "neuron", None),
            P("segment", "neuron"),
            P("segment", "neuron"),
        ),
        out_specs=P("segment", None, None, "neuron"),
        check_vma=False,
    )
```

```python
import functools

import jax
import jax.numpy as jnp
from jax import lax
from jax.experimental import pallas as pl
from jax.experimental.pallas import tpu as pltpu
from jax.sharding import PartitionSpec as P

MESH = pl.DeviceIdType.MESH
BLOCK = 128
KMAX = 5
REACH = 4
S = 128
NMB = 3
ROWS = 16
WIDE = 2 * REACH
EDGE = ROWS + 2 * REACH
XZERO = ROWS + 2 * WIDE
HZERO = EDGE
HSTEP = EDGE + 1
HALF = ROWS // 2
SAMPLES = S * NMB
AHEAD = 2
LAG = 2
SLOTS = LAG + 1


def kernel(
    segments, neurons, piece,
    samples, batch, weights, bias_any, offset_any, count_any, bias, offset, count,
    out,
    wa, wb, raw, main, halo, mid, mid_out, result, x, h, bias_l, bias_r,
    off_l, off_r, cnt_l, cnt_r, ia, ib, pos,
    load_sem, info_send, info_recv, w_send, w_recv,
    main_send, main_recv, halo_send, halo_recv, fwd_send, mid_send, mid_recv, outer_send, outer_recv, out_sem,
):
    pieces = SAMPLES // piece
    s = lax.axis_index("segment")
    n = lax.axis_index("neuron")
    left = jnp.maximum(n - 1, 0)
    right = jnp.minimum(n + 1, neurons - 1)
    there = (n > 0, n < neurons - 1)
    odd = lax.rem(s, 2)
    first = s == 0
    even = odd == 0
    last = s == segments - 1
    pair = s + 1 - 2 * odd
    crossing = jnp.logical_not(first) & jnp.logical_not(last)
    other = jnp.clip(s - 1 + 2 * odd, 0, segments - 1)

    def remote(src, dst, send, recv, device):
        return pltpu.make_async_remote_copy(
            src_ref=src, dst_ref=dst, send_sem=send, recv_sem=recv,
            device_id=device, device_id_type=MESH,
        )

    load_a = pltpu.make_async_copy(weights.at[0], wa.at[pl.ds(REACH, ROWS)], load_sem.at[0])
    load_b = pltpu.make_async_copy(weights.at[1], wb, load_sem.at[1])
    load_s = pltpu.make_async_copy(samples, raw, load_sem.at[2])
    pl.when(first)(load_s.start)
    load_a.start()
    load_b.start()

    barrier = pltpu.get_barrier_semaphore()

    def greet(device):
        pl.semaphore_signal(barrier, inc=1, device_id=device, device_id_type=MESH)

    for side, neighbour in enumerate((left, right)):

        @pl.when(there[side])
        def _():
            greet((s, neighbour))
            greet((pair, neighbour))

    greet((pair, n))
    pl.when(crossing)(lambda: greet((other, n)))

    blank = jnp.zeros((piece, BLOCK), jnp.bfloat16)
    x[XZERO] = blank
    for slot in range(SLOTS):
        h[slot * HSTEP + HZERO] = blank
    for side, (b_side, a_row) in enumerate(((bias_l, 0), (bias_r, REACH + ROWS))):

        @pl.when(jnp.logical_not(there[side]))
        def _():
            for j in range(WIDE):
                x[side * (WIDE + ROWS) + j] = blank
            for slot in range(SLOTS):
                for j in range(REACH):
                    h[slot * HSTEP + a_row + j] = blank
            b_side[...] = jnp.zeros(b_side.shape, jnp.float32)
            for j in range(REACH):
                wa[a_row + j] = jnp.zeros(wa.shape[1:], jnp.bfloat16)
                for k in range(KMAX):
                    ia[(a_row + j) * KMAX + k] = XZERO

    @pl.when(first)
    def _():
        lanes = lax.broadcasted_iota(jnp.int32, (8, SAMPLES), 0)
        hot = jnp.where(jnp.broadcast_to(batch[...].reshape(1, SAMPLES), (8, SAMPLES)) == lanes, 1.0, 0.0)
        before = jnp.where(
            lax.broadcasted_iota(jnp.int32, (SAMPLES, SAMPLES), 0)
            < lax.broadcasted_iota(jnp.int32, (SAMPLES, SAMPLES), 1),
            1.0, 0.0,
        ).astype(jnp.bfloat16)
        rank = jnp.dot(hot.astype(jnp.bfloat16), before, preferred_element_type=jnp.float32)
        place = hot * (rank + lanes.astype(jnp.float32) * float(S))
        pos[...] = jnp.broadcast_to(jnp.sum(place, axis=0, keepdims=True), (8, SAMPLES))

    greeted = 1 + crossing.astype(jnp.int32)
    for side in range(2):
        greeted = greeted + 2 * there[side].astype(jnp.int32)
    pl.semaphore_wait(barrier, greeted)

    info = [
        remote(offset_any, off_r, info_send.at[0], info_recv.at[0], (s, left)),
        remote(offset_any, off_l, info_send.at[1], info_recv.at[1], (s, right)),
        remote(count_any, cnt_r, info_send.at[2], info_recv.at[2], (s, left)),
        remote(count_any, cnt_l, info_send.at[3], info_recv.at[3], (s, right)),
        remote(bias_any, bias_r, info_send.at[4], info_recv.at[4], (s, left)),
        remote(bias_any, bias_l, info_send.at[5], info_recv.at[5], (s, right)),
    ]
    rows_of_neighbours = [
        remote(
            weights.at[0, pl.ds(0, REACH)], wa.at[pl.ds(REACH + ROWS, REACH)],
            w_send.at[0], w_recv.at[0], (s, left),
        ),
        remote(
            weights.at[0, pl.ds(ROWS - REACH, REACH)], wa.at[pl.ds(0, REACH)],
            w_send.at[1], w_recv.at[1], (s, right),
        ),
    ]

    for side in range(2):

        @pl.when(jnp.logical_not(first) & there[side])
        def _():
            for copy in info[side::2]:
                copy.start()
            rows_of_neighbours[side].start()

    def main_copy(p, half, device):
        cols = pl.ds(half * HALF * BLOCK, HALF * BLOCK)
        return remote(
            result.at[p, :, cols], main.at[p, :, cols],
            main_send.at[p, half], main_recv.at[p, half], device,
        )

    def halo_copy(p, half, device, outer):
        src = half * (ROWS - REACH) if outer else REACH + half * REACH
        send, recv = (outer_send, outer_recv) if outer else (halo_send, halo_recv)
        return remote(
            result.at[p, :, pl.ds(src * BLOCK, REACH * BLOCK)],
            halo.at[p, 1 - half, :, pl.ds((src - half * HALF) * BLOCK, REACH * BLOCK)],
            send.at[p, half], recv.at[p, 1 - half], device,
        )

    def fwd_copy(p, half, device):
        cols = pl.ds(half * HALF * BLOCK, HALF * BLOCK)
        return remote(
            main.at[p, :, cols], halo.at[p, 1 - half],
            fwd_send.at[p, half], halo_recv.at[p, 1 - half], device,
        )

    def narrow_copy(p, half, device):
        width = REACH * BLOCK
        src = pl.ds(half * (ROWS - REACH) * BLOCK, width)
        dst = pl.ds(half * REACH * BLOCK, width)
        return remote(
            main.at[p, :, src], halo.at[p, 1 - half, :, dst],
            fwd_send.at[p, half], halo_recv.at[p, 1 - half], device,
        )

    def mid_copy(p, half, device):
        return remote(
            mid_out.at[p, half], mid.at[p, 1 - half],
            mid_send.at[p, half], mid_recv.at[p, 1 - half], device,
        )

    sides = ((0, (s, left)), (1, (s, right)))
    pair_sides = ((0, (pair, left)), (1, (pair, right)))

    def prepare(p):
        @pl.when(first)
        def _():
            want = lax.broadcasted_iota(jnp.int32, (piece, SAMPLES), 0) + p * piece
            pick = jnp.where(
                jnp.broadcast_to(pos[0:1, :], (piece, SAMPLES)) == want.astype(jnp.float32),
                1.0, 0.0,
            ).astype(jnp.bfloat16)
            for c in range(0, ROWS * BLOCK, 2 * BLOCK):
                main[p, :, c : c + 2 * BLOCK] = jnp.dot(
                    pick, raw[:, c : c + 2 * BLOCK], preferred_element_type=jnp.float32
                ).astype(jnp.bfloat16)
            for half, device in sides:
                pl.when(there[half])(narrow_copy(p, half, device).start)

        @pl.when(jnp.logical_not(first))
        def _():
            for half, device in sides:
                main_copy(p, half, (s, n)).wait_recv()
                pl.when(there[half])(fwd_copy(p, half, device).start)

    def first_rows(rows, slot, keep):
        for a in rows:
            taken = jnp.concatenate([x[ia[a * KMAX + k]] for k in range(KMAX)], axis=1)
            y = jnp.dot(
                taken, wa[a].reshape(KMAX * BLOCK, BLOCK), preferred_element_type=jnp.float32
            )
            j = a - REACH
            if j < 0:
                b = bias_l[0:1, (j + ROWS) * BLOCK : (j + ROWS + 1) * BLOCK]
            elif j < ROWS:
                b = bias[0:1, j * BLOCK : (j + 1) * BLOCK]
            else:
                b = bias_r[0:1, (j - ROWS) * BLOCK : (j - ROWS + 1) * BLOCK]
            y = jnp.maximum(y + b, 0.0).astype(jnp.bfloat16)
            h[slot * HSTEP + a] = y
            if keep is not None:
                keep(j, y)

    def second_rows(rows, slot, p):
        for j in rows:
            taken = jnp.concatenate(
                [h[slot * HSTEP + ib[j * KMAX + k]] for k in range(KMAX)], axis=1
            )
            y = jnp.dot(
                taken, wb[j].reshape(KMAX * BLOCK, BLOCK), preferred_element_type=jnp.float32
            )
            b = bias[1:2, j * BLOCK : (j + 1) * BLOCK]
            result[p, :, j * BLOCK : (j + 1) * BLOCK] = jnp.maximum(y + b, 0.0).astype(jnp.bfloat16)

    def stage_a(p):
        slot = lax.rem(p, SLOTS)

        @pl.when(jnp.logical_not(even))
        def _():
            for half, _ in sides:
                main_copy(p, half, (pair, n)).wait_recv()

        for j in range(ROWS):
            x[WIDE + j] = main[p, :, j * BLOCK : (j + 1) * BLOCK]
        first_rows(range(2 * REACH, EDGE - 2 * REACH), slot, None)
        relays = even & jnp.logical_not(first) & (p + AHEAD < pieces)
        pl.when(relays)(lambda: prepare(p + AHEAD))

        @pl.when(first)
        def _():
            @pl.when(there[0])
            def _():
                narrow_copy(p, 1, (s, left)).wait_recv()
                for j in range(REACH, WIDE):
                    x[j] = halo[p, 0, :, j * BLOCK : (j + 1) * BLOCK]

            @pl.when(there[1])
            def _():
                narrow_copy(p, 0, (s, right)).wait_recv()
                for j in range(REACH):
                    x[WIDE + ROWS + j] = halo[p, 1, :, j * BLOCK : (j + 1) * BLOCK]

            def keep(j, y):
                half = 0 if j < REACH else 1
                c = (j - half * (ROWS - REACH)) * BLOCK
                mid_out[p, half, :, c : c + BLOCK] = y

            first_rows(range(REACH, 2 * REACH), slot, keep)
            first_rows(range(EDGE - 2 * REACH, EDGE - REACH), slot, keep)
            for half, device in sides:
                pl.when(there[half])(mid_copy(p, half, device).start)

        @pl.when(jnp.logical_not(first))
        def _():
            for side in range(2):

                @pl.when(there[side])
                def _():
                    pl.when(even)(fwd_copy(p, 1 - side, sides[side][1]).wait_recv)

                    @pl.when(jnp.logical_not(even))
                    def _():
                        for outer in (True, False):
                            halo_copy(p, 1 - side, pair_sides[side][1], outer).wait_recv()

                    for j in range(WIDE):
                        x[side * (WIDE + ROWS) + j] = halo[p, side, :, j * BLOCK : (j + 1) * BLOCK]
            first_rows(range(2 * REACH), slot, None)
            first_rows(range(EDGE - 2 * REACH, EDGE), slot, None)

    def stage_b(p):
        slot = lax.rem(p, SLOTS)

        @pl.when(first)
        def _():
            for side in range(2):

                @pl.when(there[side])
                def _():
                    mid_copy(p, 1 - side, sides[side][1]).wait_recv()
                    for j in range(REACH):
                        h[slot * HSTEP + side * (REACH + ROWS) + j] = mid[
                            p, side, :, j * BLOCK : (j + 1) * BLOCK
                        ]

        @pl.when(even)
        def _():
            ends = [*range(REACH), *range(ROWS - REACH, ROWS)]
            for rows, outer in ((ends, True), (range(REACH, ROWS - REACH), False)):
                second_rows(rows, slot, p)
                for half, device in pair_sides:
                    pl.when(there[half])(halo_copy(p, half, device, outer).start)
            for half in range(2):
                main_copy(p, half, (pair, n)).start()

        @pl.when(jnp.logical_not(even))
        def _():
            for half in range(2):
                second_rows(range(half * HALF, (half + 1) * HALF), slot, p)
                pl.when(jnp.logical_not(last))(main_copy(p, half, (other, n)).start)

        out_copy(p).start()

    def out_copy(p):
        return pltpu.make_async_copy(
            result.at[p], out.at[pl.ds(p * piece, piece), :], out_sem.at[p]
        )

    def fill(table, entry, off_ref, cnt_ref, layer, row, j, base, zero):
        used = cnt_ref[layer, row]
        for k in range(KMAX):
            off = off_ref[k, layer, row]
            place = n * ROWS + j + off
            live = (k < used) & (place >= 0) & (place < neurons * ROWS)
            table[entry * KMAX + k] = jnp.where(live, base + j + off, zero)

    def own(r, carry):
        fill(ia, r + REACH, offset, count, 0, r, r, WIDE, XZERO)
        fill(ib, r, offset, count, 1, r, r, REACH, HZERO)
        return carry

    @pl.when(first)
    def _():
        load_s.wait()
        for p in range(AHEAD):
            prepare(p)

    lax.fori_loop(0, ROWS, own, 0)

    @pl.when(jnp.logical_not(first))
    def _():
        for side, (off_side, cnt_side, row) in enumerate(
            ((off_l, cnt_l, ROWS - REACH), (off_r, cnt_r, 0))
        ):

            @pl.when(there[side])
            def _():
                for copy in info[1 - side :: 2]:
                    copy.wait_recv()

                def side_row(r, carry):
                    j = r - REACH + side * (REACH + ROWS)
                    fill(ia, j + REACH, off_side, cnt_side, 0, row + r, j, WIDE, XZERO)
                    return carry

                lax.fori_loop(0, REACH, side_row, 0)
                rows_of_neighbours[1 - side].wait_recv()

    load_a.wait()
    load_b.wait()

    @pl.when(even & jnp.logical_not(first))
    def _():
        for p in range(AHEAD):
            prepare(p)

    def step(q, carry):
        @pl.when(q < pieces)
        def _():
            pl.when(first & (q + AHEAD < pieces))(lambda: prepare(q + AHEAD))
            stage_a(q)

        p = q - jnp.where(first, LAG, 0)
        pl.when((p >= 0) & (p < pieces))(lambda: stage_b(p))
        return carry

    lax.fori_loop(0, pieces + LAG, step, 0)

    for side in range(2):

        @pl.when(jnp.logical_not(first) & there[side])
        def _():
            for copy in info[side::2]:
                copy.wait_send()
            rows_of_neighbours[side].wait_send()

    def drain(p, carry):
        out_copy(p).wait()
        for half in range(2):
            pl.when(jnp.logical_not(last))(lambda: main_copy(p, half, (pair, n)).wait_send())

            @pl.when(there[half])
            def _():
                for outer in (True, False):
                    pl.when(even)(
                        lambda: halo_copy(p, half, pair_sides[half][1], outer).wait_send()
                    )
                pl.when(first)(lambda: narrow_copy(p, half, sides[half][1]).wait_send())
                pl.when(first)(lambda: mid_copy(p, half, sides[half][1]).wait_send())
                pl.when(even & jnp.logical_not(first))(
                    lambda: fwd_copy(p, half, sides[half][1]).wait_send()
                )

        return carry

    lax.fori_loop(0, pieces, drain, 0)


def solution(mesh):
    segments, neurons = mesh.shape["segment"], mesh.shape["neuron"]
    piece = 48
    pieces = SAMPLES // piece
    width = ROWS * BLOCK
    bf16, f32, i32 = jnp.bfloat16, jnp.float32, jnp.int32

    def on_device(samples, batch_of, weights, block_offset, block_count, bias):
        dma = pltpu.SemaphoreType.DMA
        vmem = pl.BlockSpec(memory_space=pltpu.VMEM)
        smem = pl.BlockSpec(memory_space=pltpu.SMEM)
        hbm = pl.BlockSpec(memory_space=pl.ANY)
        offset = block_offset.transpose(2, 0, 1)
        result = pl.pallas_call(
            functools.partial(kernel, segments, neurons, piece),
            out_shape=jax.ShapeDtypeStruct((SAMPLES, width), bf16),
            in_specs=[hbm, vmem, hbm, hbm, hbm, hbm, vmem, smem, smem],
            out_specs=hbm,
            scratch_shapes=[
                pltpu.VMEM((EDGE, KMAX, BLOCK, BLOCK), bf16),
                pltpu.VMEM((ROWS, KMAX, BLOCK, BLOCK), bf16),
                pltpu.VMEM((SAMPLES, width), bf16),
                pltpu.VMEM((pieces, piece, width), bf16),
                pltpu.VMEM((pieces, 2, piece, WIDE * BLOCK), bf16),
                pltpu.VMEM((pieces, 2, piece, REACH * BLOCK), bf16),
                pltpu.VMEM((pieces, 2, piece, REACH * BLOCK), bf16),
                pltpu.VMEM((pieces, piece, width), bf16),
                pltpu.VMEM((XZERO + 1, piece, BLOCK), bf16),
                pltpu.VMEM((SLOTS * HSTEP, piece, BLOCK), bf16),
                pltpu.VMEM(bias.shape, f32),
                pltpu.VMEM(bias.shape, f32),
                pltpu.SMEM(offset.shape, i32),
                pltpu.SMEM(offset.shape, i32),
                pltpu.SMEM(block_count.shape, i32),
                pltpu.SMEM(block_count.shape, i32),
                pltpu.SMEM((EDGE * KMAX,), i32),
                pltpu.SMEM((ROWS * KMAX,), i32),
                pltpu.VMEM((8, SAMPLES), f32),
                dma((3,)), dma((6,)), dma((6,)), dma((2,)), dma((2,)),
                dma((pieces, 2)), dma((pieces, 2)), dma((pieces, 2)), dma((pieces, 2)),
                dma((pieces, 2)), dma((pieces, 2)), dma((pieces, 2)), dma((pieces, 2)), dma((pieces, 2)),
                dma((pieces,)),
            ],
            compiler_params=pltpu.CompilerParams(
                collective_id=0, has_side_effects=True, vmem_limit_bytes=56 << 20
            ),
        )(
            samples, batch_of, weights, bias, offset, block_count,
            bias, offset, block_count,
        )
        return result.reshape(1, NMB, S, width)

    return jax.shard_map(
        on_device,
        mesh=mesh,
        in_specs=(
            P(None, "neuron"),
            P(),
            P("segment", "neuron", None, None, None),
            P("segment", "neuron", None),
            P("segment", "neuron"),
            P("segment", "neuron"),
        ),
        out_specs=P("segment", None, None, "neuron"),
        check_vma=False,
    )
```
